768 devices in a mesh: rep: 12 (over x, z_lo), fsdp: 64 (over z_hi, y, core).
Axes of the slice: x: 4, y: 8, z: 12 (z_hi: 4, z_lo: 3; z = z_hi * 3 + z_lo), core: 2. Of those that a mesh axis runs over, the one named last changes fastest.
Arguments:
- gate_pre: bfloat16 [6144, 12288], P('rep', 'fsdp'), may hold values from -6 to 6
- up_pre: bfloat16 [6144, 12288], P('rep', 'fsdp'), may hold values from -40 to 40
- out_grad: bfloat16 [6144, 3072], P('rep'), may hold values from -6 to 6
- inner_params: bfloat16 [12, 12288, 3072], P('rep', 'fsdp'), may hold values from -0.109375 to 0.109375
- global_params: float32 [12288, 3072], P('fsdp', 'rep'), may hold values from -0.109375 to 0.109375
- outer_momentum: float32 [12288, 3072], P('fsdp', 'rep'), may hold values from -0.15625 to 0.15625
- pair_codes: int32 [12, 12288, 1536], P('rep', 'fsdp'), may hold values from 0 to 255
- code_scales: float32 [12, 12288, 24], P('rep', 'fsdp'), may hold values from 0.001 to 0.01
Outputs:
- merged_params: bfloat16 [12, 12288, 3072], P('rep', 'fsdp')
- new_global: float32 [12288, 3072], P('fsdp', 'rep')
- new_momentum: float32 [12288, 3072], P('fsdp', 'rep')
The draws below stay inside these ranges and needn't reach their ends.
Inputs may be any that keep to these rules, and one draw needn't show every extreme that they name: `pair_codes`: each word holds two codes of 0 to 15: its value mod 16 for column 2 j and its value // 16 for column 2 j + 1.
All inputs are finite; a program needn't handle non-finite values.
Results may differ from the reference program's by a relative error of at most 0.011.
Values may be sent and summed in bfloat16 or wider, within the bound.
No kernel may reach another device: no remote copies, remote signals or barrier semaphores. Data moves between devices by JAX's collectives and lax.ppermute only.
A program may use at most 64 MiB of HBM per device.

```python
import math
import jax
import jax.numpy as jnp
from jax import lax

D = 3072
UNITS = 12288
BLOCK = 128
TOK_REP = 512
TOKENS = 6144
N_REP = 12


def draw_up_pre(key, part):
    key = jax.random.fold_in(key, 5)
    base_key, rough_key = jax.random.split(key)
    column = jnp.arange(UNITS, dtype=jnp.float32) / UNITS
    rough = jnp.exp(jax.random.uniform(rough_key, (UNITS,), jnp.float32, 0.0, 0.7))
    base = jnp.clip(jax.random.normal(base_key, (TOKENS, UNITS), jnp.float32), -6.0, 6.0)
    rising = 10.0 ** (column - 0.5)
    return (base * (rising * rough)[None, :]).astype(jnp.bfloat16)


def plant(array, own_key, least, top_value):
    longest = array.shape.index(max(array.shape))
    spots = []
    for shift in (0, 1):
        where = [jax.random.randint(jax.random.fold_in(own_key, axis), (), 0, length) for axis, length in enumerate(array.shape)]
        where[longest] = (where[longest] + shift) % array.shape[longest]
        spots.append(tuple(where))
    return array.at[spots[0]].set(least).at[spots[1]].set(top_value)


def shard_levels(key, dims, shards, smallest, top_value):
    factor_of, own = 1.0, jax.random.fold_in(key, 6)
    for axis_at, shards_of in shards:
        steps = jnp.exp(jax.random.uniform(jax.random.fold_in(own, axis_at), (shards_of,), jnp.float32, smallest / len(shards), top_value / len(shards)))
        factor_of = factor_of * jnp.repeat(steps, dims[axis_at] // shards_of).reshape([-1 if axis == axis_at else 1 for axis in range(len(dims))])
    return factor_of


def gaussian(rng, extent, deviation, bound, pieces=(), held_as=jnp.bfloat16):
    array = jax.random.normal(rng, extent, jnp.float32) * deviation
    if len(pieces) > 0:
        array = shard_levels(rng, extent, pieces, -0.22, 0.18) * array
    return jnp.clip(array, min=-bound, max=bound).astype(held_as)


def setup_inputs(seed: int = 0) -> dict:
    splits = jax.random.split(jax.random.key(seed), 9)
    gate_pre = gaussian(splits[0], (TOKENS, UNITS), 1.0, 6.0, ((0, 12), (1, 64)))
    up_pre = draw_up_pre(jax.random.fold_in(splits[8], 71), 0)
    out_grad = gaussian(splits[2], (TOKENS, D), 1.0, 6.0, ((0, 12),))
    inner_params = gaussian(splits[3], (N_REP, UNITS, D), D ** -0.5, 0.109375, ((0, 12), (1, 64)))
    global_params = gaussian(splits[4], (UNITS, D), D ** -0.5, 0.109375, ((0, 64), (1, 12)), jnp.float32)
    outer_momentum = gaussian(splits[5], (UNITS, D), 0.01, 0.15625, ((0, 64), (1, 12)), jnp.float32)
    pair_codes = plant(jax.random.randint(splits[6], (N_REP, UNITS, D // 2), 0, 256), jax.random.fold_in(splits[6], 1), 0, 255).astype(jnp.int32)
    code_scales = jnp.clip(jnp.exp(math.log(0.01) - 2.30258502 * jax.random.uniform(splits[7], (N_REP, UNITS, D // BLOCK), jnp.float32) ** shard_levels(splits[7], (N_REP, UNITS, D // BLOCK), ((0, 12), (1, 64)), -0.2, 0.2)), 0.001, 0.01)
    return dict(gate_pre=gate_pre, up_pre=up_pre, out_grad=out_grad, inner_params=inner_params, global_params=global_params, outer_momentum=outer_momentum, pair_codes=pair_codes, code_scales=code_scales)


def unpack(packed, scales):
    lower_code = packed % 16
    upper_code = packed // 16
    unpacked = jnp.stack([lower_code, upper_code], axis=-1).reshape(packed.shape[:-1] + (2 * packed.shape[-1],))
    centered = (unpacked - 8).astype(jnp.float32)
    blocks = centered.reshape(packed.shape[:-1] + (scales.shape[-1], -1)) * scales[..., None]
    return blocks.reshape(unpacked.shape).astype(jnp.bfloat16)

def reference(gate_pre, up_pre, out_grad, inner_params, global_params, outer_momentum, pair_codes, code_scales):

    def add_replica(running, item_pair):
        return (running + unpack(item_pair[0], item_pair[1]).astype(jnp.float32), None)
    running, _ = lax.scan(add_replica, jnp.zeros((UNITS, D), jnp.float32), (pair_codes, code_scales))
    mean_delta = running * (1.0 / N_REP)
    new_momentum = 0.9 * outer_momentum + mean_delta
    new_global = global_params - 0.7 * (mean_delta + 0.9 * new_momentum)
    global_bf = lax.optimization_barrier(new_global.astype(jnp.bfloat16)).astype(jnp.float32)
    gate_f32 = gate_pre.astype(jnp.float32)
    upper = up_pre.astype(jnp.float32)
    sigmoid_gate = jax.nn.sigmoid(gate_f32)
    hidden = (gate_f32 * sigmoid_gate * upper).astype(jnp.bfloat16)
    hidden_rows = hidden.reshape(N_REP, TOK_REP, UNITS)
    grad_rows = out_grad.reshape(N_REP, TOK_REP, D)

    def one_replica(replica_items):
        hidden_part, grad_part, params = replica_items
        grads = jnp.dot(hidden_part.T, grad_part, preferred_element_type=jnp.float32) * (1.0 / TOK_REP)
        root_mean = jnp.sqrt(jnp.sum(grads * grads) / (UNITS * D) + 1e-06)
        clipped = grads * jnp.minimum(1.0, 0.02 / root_mean)
        master = params.astype(jnp.float32)
        stepped = master - 0.8 * (clipped + 0.2 * master)
        return (0.5 * stepped + 0.5 * global_bf).astype(jnp.bfloat16)
    merged_params = lax.map(one_replica, (hidden_rows, grad_rows, inner_params))
    return (merged_params, new_global, new_momentum)
```

```python
import jax
import jax.numpy as jnp
from jax import lax
from jax.experimental import pallas as pl
from jax.experimental.pallas import tpu as pltpu
from jax.sharding import Mesh, PartitionSpec as P

REP = ("x", "zl")
FSDP = ("zh", "y", "core")
VMEM_BYTES = 32 * 1024 * 1024


def unpack_kernel(words_ref, scales_ref, out_ref):
    scales = scales_ref[...].T
    first = lax.broadcasted_iota(jnp.int32, (words_ref.shape[0], 128), 1) < 64
    for c in range(out_ref.shape[0]):
        words = words_ref[:, c * 128 : (c + 1) * 128]
        scale = jnp.where(first, scales[:, 2 * c : 2 * c + 1], scales[:, 2 * c + 1 : 2 * c + 2])
        low = ((words & 15) - 8).astype(jnp.float32) * scale
        high = ((words >> 4) - 8).astype(jnp.float32) * scale
        out_ref[c, :, :128] = low.astype(jnp.bfloat16)
        out_ref[c, :, 128:] = high.astype(jnp.bfloat16)


def unpack(words, scales_t, parts):
    rows = words.shape[0]
    return pl.pallas_call(
        unpack_kernel,
        out_shape=jax.ShapeDtypeStruct((parts, rows, 256), jnp.bfloat16),
        compiler_params=pltpu.CompilerParams(vmem_limit_bytes=VMEM_BYTES),
        name="unpack",
    )(words, scales_t)


def grads_kernel(gate_ref, up_ref, out_grad_ref, grads_ref, total_ref):
    gate = gate_ref[...].astype(jnp.float32)
    up = up_ref[...].astype(jnp.float32)
    hidden = (gate * jax.nn.sigmoid(gate) * up).astype(jnp.bfloat16)
    tokens = gate_ref.shape[1]
    width = out_grad_ref.shape[1]
    total = jnp.zeros((8, 512), jnp.float32)
    for c in range(0, width, 512):
        part = lax.dot_general(
            hidden,
            out_grad_ref[:, c : c + 512],
            (((1,), (0,)), ((), ())),
            preferred_element_type=jnp.float32,
        ) * (1.0 / tokens)
        grads_ref[:, c : c + 512] = part
        total += jnp.sum((part * part).reshape(-1, 8, 512), axis=0)
    total_ref[...] = jnp.broadcast_to(jnp.sum(total), (8, 128))


def gradients(gate_t, up_t, out_grad):
    rows = gate_t.shape[0]
    width = out_grad.shape[1]
    return pl.pallas_call(
        grads_kernel,
        out_shape=(
            jax.ShapeDtypeStruct((rows, width), jnp.float32),
            jax.ShapeDtypeStruct((8, 128), jnp.float32),
        ),
        compiler_params=pltpu.CompilerParams(vmem_limit_bytes=VMEM_BYTES),
        cost_estimate=pl.CostEstimate(
            flops=2 * rows * width * gate_t.shape[1], bytes_accessed=6_000_000, transcendentals=100_000
        ),
        name="gradients",
    )(gate_t, up_t, out_grad)


def update_kernel(replicas, parts_ref, momentum_ref, params_ref, global_ref, momentum_out_ref, bf_ref):
    row = lax.broadcasted_iota(jnp.int32, (256, 256), 0)
    col = lax.broadcasted_iota(jnp.int32, (256, 256), 1)
    weave = ((row & 127) * 2 + (row >> 7) == col).astype(jnp.bfloat16)
    delta = jnp.zeros(momentum_ref.shape, jnp.float32)
    for c in range(parts_ref.shape[0]):
        delta += jnp.dot(parts_ref[c], weave, preferred_element_type=jnp.float32)
    delta = delta * (1.0 / replicas)
    momentum = 0.9 * momentum_ref[...] + delta
    new_global = params_ref[...] - 0.7 * (delta + 0.9 * momentum)
    momentum_out_ref[...] = momentum
    global_ref[...] = new_global
    bf = new_global.astype(jnp.bfloat16)
    for c in range(bf_ref.shape[0]):
        bf_ref[c] = bf


def update(parts, momentum, params):
    shape = jax.ShapeDtypeStruct(momentum.shape, jnp.float32)
    import functools
    return pl.pallas_call(
        functools.partial(update_kernel, parts.shape[0]),
        out_shape=(shape, shape, jax.ShapeDtypeStruct(parts.shape, jnp.bfloat16)),
        compiler_params=pltpu.CompilerParams(vmem_limit_bytes=VMEM_BYTES),
        name="update",
    )(parts, momentum, params)


def merge_kernel(total_ref, grads_ref, inner_ref, global_ref, out_ref):
    entries = 12288 * 3072
    root_mean = jnp.sqrt(total_ref[:1, :1] / entries + 1e-6)
    clip = jnp.minimum(1.0, 0.02 / root_mean)
    for c in range(global_ref.shape[0]):
        cols = slice(c * 256, (c + 1) * 256)
        clipped = grads_ref[:, cols] * clip
        master = inner_ref[:, cols].astype(jnp.float32)
        stepped = master - 0.8 * (clipped + 0.2 * master)
        out_ref[:, cols] = (0.5 * stepped + 0.5 * global_ref[c].astype(jnp.float32)).astype(jnp.bfloat16)


def merge(total, grads, inner, global_parts):
    return pl.pallas_call(
        merge_kernel,
        out_shape=jax.ShapeDtypeStruct(inner.shape, jnp.bfloat16),
        compiler_params=pltpu.CompilerParams(vmem_limit_bytes=VMEM_BYTES),
        name="merge",
    )(total, grads, inner, global_parts)


def per_device(gate_pre, up_pre, out_grad, inner_params, global_params, outer_momentum, pair_codes, code_scales):
    replicas = lax.axis_size(REP)
    pseudo = unpack(pair_codes[0], code_scales[0].T, replicas)
    parts = lax.all_to_all(pseudo, REP, 0, 0, tiled=True)
    grads, total = gradients(gate_pre.T, up_pre.T, out_grad)
    for axis in ("core", "y", "zh"):
        total = lax.psum(total, axis)
    new_global, new_momentum, global_bf = update(parts, outer_momentum, global_params)
    global_parts = lax.all_to_all(global_bf, REP, 0, 0, tiled=True)
    merged = merge(total, grads, inner_params[0], global_parts)
    return (merged[None], new_global, new_momentum)


def solution(mesh):
    fine = Mesh(mesh.devices.reshape(4, 3, 4, 8, 2), REP + FSDP)
    in_specs = (
        P(REP, FSDP),
        P(REP, FSDP),
        P(REP, None),
        P(REP, FSDP, None),
        P(FSDP, REP),
        P(FSDP, REP),
        P(REP, FSDP, None),
        P(REP, FSDP, None),
    )
    out_specs = (P(REP, FSDP, None), P(FSDP, REP), P(FSDP, REP))
    return jax.shard_map(
        per_device, mesh=fine, in_specs=in_specs, out_specs=out_specs, check_vma=False
    )
```

```python
import jax
import jax.numpy as jnp
from jax import lax
from jax.experimental import pallas as pl
from jax.experimental.pallas import tpu as pltpu
from jax.sharding import Mesh, PartitionSpec as P

REP = ("x", "zl")
FSDP = ("zh", "y", "core")
REPLICAS = 12
ENTRIES = 12288 * 3072
MIB = 1024 * 1024
ANY = pl.BlockSpec(memory_space=pl.ANY)


def hbm(x):
    return pltpu.with_memory_space_constraint(x, pltpu.HBM)


def unpack_kernel(words_hbm, scales_hbm, out_hbm, order_ref, words_ref, scales_ref, out_ref, sems):
    steps, per_step, rows, _ = out_ref.shape
    span = per_step * 128
    copies_in = [pltpu.make_async_copy(scales_hbm, scales_ref, sems.at[0])]
    for i in range(steps):
        cols = pl.ds(i * span, span)
        copies_in.append(
            pltpu.make_async_copy(words_hbm.at[:, cols], words_ref.at[:, cols], sems.at[1 + i])
        )
    for copy in copies_in:
        copy.start()
    order_ref[...] = jnp.zeros(order_ref.shape, jnp.float32)
    first = lax.broadcasted_iota(jnp.int32, (rows, 128), 1) < 64
    copies_in[0].wait()
    scales = scales_ref[...].T
    copies_out = []
    for i in range(steps):
        copies_in[1 + i].wait()
        for k in range(per_step):
            c = i * per_step + k
            words = words_ref[:, c * 128 : (c + 1) * 128]
            scale = jnp.where(first, scales[:, 2 * c : 2 * c + 1], scales[:, 2 * c + 1 : 2 * c + 2])
            low = ((words & 15) - 8).astype(jnp.float32) * scale
            high = ((words >> 4) - 8).astype(jnp.float32) * scale
            out_ref[i, k, :, :128] = low.astype(jnp.bfloat16)
            out_ref[i, k, :, 128:] = high.astype(jnp.bfloat16)
        copies_out.append(pltpu.make_async_copy(out_ref.at[i], out_hbm.at[i], sems.at[1 + steps + i]))
        copies_out[-1].start()
    for copy in copies_out:
        copy.wait()


def unpack(words, scales_t):
    rows, width = words.shape
    shape = (4, REPLICAS // 4, rows, 256)
    return pl.pallas_call(
        unpack_kernel,
        in_specs=[ANY, ANY],
        out_specs=(ANY, pl.BlockSpec(memory_space=pltpu.VMEM)),
        out_shape=(
            pltpu.HBM(shape, jnp.bfloat16),
            pltpu.VMEM((8, 128), jnp.float32),
        ),
        scratch_shapes=[
            pltpu.VMEM((rows, width), jnp.int32),
            pltpu.VMEM(scales_t.shape, jnp.float32),
            pltpu.VMEM(shape, jnp.bfloat16),
            pltpu.SemaphoreType.DMA((9,)),
        ],
        compiler_params=pltpu.CompilerParams(vmem_limit_bytes=32 * MIB),
        name="unpack",
    )(hbm(words), hbm(scales_t))


def gradients_kernel(
    order_ref, gate_hbm, up_hbm, out_grad_hbm, momentum_hbm, params_hbm,
    grads_ref, total_ref, momentum_ref, params_ref,
    gate_ref, up_ref, out_grad_ref, sems,
):
    width = out_grad_ref.shape[1]
    steps = width // 512
    columns = [pl.ds(c * 512, 512) for c in range(steps)]
    first = [
        pltpu.make_async_copy(gate_hbm, gate_ref, sems.at[0]),
        pltpu.make_async_copy(up_hbm, up_ref, sems.at[1]),
    ]
    blocks = [
        pltpu.make_async_copy(out_grad_hbm.at[:, cols], out_grad_ref.at[:, cols], sems.at[2 + c])
        for c, cols in enumerate(columns)
    ]
    last = [
        pltpu.make_async_copy(momentum_hbm, momentum_ref, sems.at[2 + steps]),
        pltpu.make_async_copy(params_hbm, params_ref, sems.at[3 + steps]),
    ]
    for copy in first + blocks + last:
        copy.start()
    for copy in first:
        copy.wait()
    gate = gate_ref[...].astype(jnp.float32)
    up = up_ref[...].astype(jnp.float32)
    hidden = (gate * jax.nn.sigmoid(gate) * up).astype(jnp.bfloat16)
    tokens = gate_ref.shape[1]
    total = jnp.zeros((8, 512), jnp.float32)
    for copy, cols in zip(blocks, columns):
        copy.wait()
        part = lax.dot_general(
            hidden, out_grad_ref[:, cols], (((1,), (0,)), ((), ())), preferred_element_type=jnp.float32
        ) * (1.0 / tokens)
        grads_ref[:, cols] = part.astype(jnp.bfloat16)
        total += jnp.sum((part * part).reshape(-1, 8, 512), axis=0)
    total_ref[...] = jnp.broadcast_to(jnp.sum(total), (8, 128)) + order_ref[...]
    for copy in last:
        copy.wait()


def gradients(order, gate_t, up_t, out_grad, momentum, params):
    rows, tokens = gate_t.shape
    width = out_grad.shape[1]
    state = pltpu.VMEM(momentum.shape, jnp.float32)
    return pl.pallas_call(
        gradients_kernel,
        in_specs=[pl.BlockSpec(memory_space=pltpu.VMEM)] + [ANY] * 5,
        out_shape=(
            pltpu.VMEM((rows, width), jnp.bfloat16),
            pltpu.VMEM((8, 128), jnp.float32),
            state,
            state,
        ),
        scratch_shapes=[
            pltpu.VMEM((rows, tokens), jnp.bfloat16),
            pltpu.VMEM((rows, tokens), jnp.bfloat16),
            pltpu.VMEM((tokens, width), jnp.bfloat16),
            pltpu.SemaphoreType.DMA((width // 512 + 4,)),
        ],
        compiler_params=pltpu.CompilerParams(vmem_limit_bytes=32 * MIB),
        cost_estimate=pl.CostEstimate(
            flops=2 * rows * width * tokens, bytes_accessed=6_000_000, transcendentals=rows * tokens
        ),
        name="gradients",
    )(order, *map(hbm, (gate_t, up_t, out_grad, momentum, params)))


def update_kernel(parts_ref, momentum_ref, params_ref, total_ref, bf_hbm, delta_ref, total_out_ref, bf_ref, sems):
    row = lax.broadcasted_iota(jnp.int32, (256, 256), 0)
    col = lax.broadcasted_iota(jnp.int32, (256, 256), 1)
    weave = ((row & 127) * 2 + (row >> 7) == col).astype(jnp.bfloat16)
    delta = jnp.zeros(momentum_ref.shape, jnp.float32)
    for c in range(parts_ref.shape[0]):
        delta += jnp.dot(parts_ref[c], weave, preferred_element_type=jnp.float32)
    delta = delta * (1.0 / REPLICAS)
    momentum = 0.9 * momentum_ref[...] + delta
    new_global = params_ref[...] - 0.7 * (delta + 0.9 * momentum)
    bf_ref[...] = new_global.astype(jnp.bfloat16)
    copies = [pltpu.make_async_copy(bf_ref, bf_hbm.at[c], sems.at[c]) for c in range(bf_hbm.shape[0])]
    for copy in copies:
        copy.start()
    delta_ref[...] = delta
    total_out_ref[...] = total_ref[...]
    for copy in copies:
        copy.wait()


def update(parts, momentum, params, total):
    rows, width = momentum.shape
    vmem = pl.BlockSpec(memory_space=pltpu.VMEM)
    return pl.pallas_call(
        update_kernel,
        out_specs=(ANY, vmem, vmem),
        out_shape=(
            pltpu.HBM((3, rows, width), jnp.bfloat16),
            pltpu.HBM((rows, width), jnp.float32),
            pltpu.VMEM((8, 128), jnp.float32),
        ),
        scratch_shapes=[pltpu.VMEM((rows, width), jnp.bfloat16), pltpu.SemaphoreType.DMA((3,))],
        compiler_params=pltpu.CompilerParams(vmem_limit_bytes=32 * MIB),
        name="update",
    )(parts, momentum, params, total)


def repeat_kernel(block_ref, total_ref, out_hbm, total_out_ref, sems):
    copies = [pltpu.make_async_copy(block_ref, out_hbm.at[i], sems.at[i]) for i in range(out_hbm.shape[0])]
    for copy in copies:
        copy.start()
    total_out_ref[...] = total_ref[...]
    for copy in copies:
        copy.wait()


def repeat(block, total):
    vmem = pl.BlockSpec(memory_space=pltpu.VMEM)
    return pl.pallas_call(
        repeat_kernel,
        out_specs=(ANY, vmem),
        out_shape=(
            pltpu.HBM((4,) + block.shape, block.dtype),
            pltpu.VMEM((8, 128), jnp.float32),
        ),
        scratch_shapes=[pltpu.SemaphoreType.DMA((4,))],
        compiler_params=pltpu.CompilerParams(vmem_limit_bytes=32 * MIB),
        name="repeat",
    )(block, total)


def state_kernel(total_ref, delta_hbm, momentum_hbm, params_hbm, inner_hbm,
                 global_ref, momentum_out_ref, inner_ref, total_out_ref,
                 delta_ref, momentum_ref, params_ref, sems):
    pairs = [
        (delta_hbm, delta_ref), (momentum_hbm, momentum_ref), (params_hbm, params_ref), (inner_hbm, inner_ref)
    ]
    copies = [pltpu.make_async_copy(src, dst, sems.at[i]) for i, (src, dst) in enumerate(pairs)]
    for copy in copies:
        copy.start()
    total_out_ref[...] = total_ref[...]
    for copy in copies[:3]:
        copy.wait()
    momentum = 0.9 * momentum_ref[...] + delta_ref[...]
    momentum_out_ref[...] = momentum
    global_ref[...] = params_ref[...] - 0.7 * (delta_ref[...] + 0.9 * momentum)
    copies[3].wait()


def state(delta, momentum, params, total, inner):
    shape = jax.ShapeDtypeStruct(momentum.shape, jnp.float32)
    block = pltpu.VMEM(momentum.shape, jnp.float32)
    return pl.pallas_call(
        state_kernel,
        in_specs=[pl.BlockSpec(memory_space=pltpu.VMEM)] + [ANY] * 4,
        out_shape=(
            shape,
            shape,
            pltpu.VMEM(inner.shape, inner.dtype),
            pltpu.VMEM((8, 128), jnp.float32),
        ),
        scratch_shapes=[block, block, block, pltpu.SemaphoreType.DMA((4,))],
        compiler_params=pltpu.CompilerParams(vmem_limit_bytes=32 * MIB),
        name="state",
    )(total, *map(hbm, (delta, momentum, params, inner)))


def merge_kernel(total_ref, grads_ref, inner_ref, global_ref, out_hbm, out_ref, sems):
    root_mean = jnp.sqrt(total_ref[:1, :1] / ENTRIES + 1e-6)
    clip = jnp.minimum(1.0, 0.02 / root_mean)
    copies = []
    for c in range(REPLICAS):
        cols = pl.ds(c * 256, 256)
        clipped = grads_ref[:, cols].astype(jnp.float32) * clip
        master = inner_ref[:, cols].astype(jnp.float32)
        stepped = master - 0.8 * (clipped + 0.2 * master)
        mean = 0.5 * stepped + 0.5 * global_ref[c].astype(jnp.float32)
        out_ref[:, cols] = mean.astype(jnp.bfloat16)
        if c % 3 == 2:
            cols = pl.ds((c - 2) * 256, 768)
            copies.append(pltpu.make_async_copy(out_ref.at[:, cols], out_hbm.at[:, cols], sems.at[c // 3]))
            copies[-1].start()
    for copy in copies:
        copy.wait()


def merge(total, grads, inner, global_parts):
    return pl.pallas_call(
        merge_kernel,
        out_specs=ANY,
        out_shape=jax.ShapeDtypeStruct(inner.shape, jnp.bfloat16),
        scratch_shapes=[pltpu.VMEM(inner.shape, jnp.bfloat16), pltpu.SemaphoreType.DMA((4,))],
        compiler_params=pltpu.CompilerParams(vmem_limit_bytes=32 * MIB),
        name="merge",
    )(total, grads, inner, global_parts)


def per_device(gate_pre, up_pre, out_grad, inner_params, global_params, outer_momentum, pair_codes, code_scales):
    pseudo, order = unpack(pair_codes[0], code_scales[0].T)
    grads, total, momentum, params = gradients(order, gate_pre.T, up_pre.T, out_grad, outer_momentum, global_params)
    parts = lax.all_to_all(pseudo.reshape((REPLICAS,) + pseudo.shape[2:]), REP, 0, 0, tiled=True)
    total = lax.psum(total, "y")
    global_bf, delta, total = update(parts, momentum, params, total)
    run_parts = lax.all_to_all(global_bf, "zl", 0, 0, tiled=True)
    total = lax.psum(total, "core")
    new_global, new_momentum, inner, total = state(delta, outer_momentum, global_params, total, inner_params[0])
    run_parts, total = repeat(run_parts, total)
    global_parts = lax.all_to_all(run_parts, "x", 0, 0, tiled=True)
    total = lax.psum(total, "zh")
    merged = merge(total, grads, inner, global_parts.reshape((REPLICAS,) + global_parts.shape[2:]))
    return (merged[None], new_global, new_momentum)


def solution(mesh):
    fine = Mesh(mesh.devices.reshape(4, 3, 4, 8, 2), REP + FSDP)
    in_specs = (
        P(REP, FSDP),
        P(REP, FSDP),
        P(REP, None),
        P(REP, FSDP, None),
        P(FSDP, REP),
        P(FSDP, REP),
        P(REP, FSDP, None),
        P(REP, FSDP, None),
    )
    out_specs = (P(REP, FSDP, None), P(FSDP, REP), P(FSDP, REP))
    return jax.shard_map(
        per_device, mesh=fine, in_specs=in_specs, out_specs=out_specs, check_vma=False
    )
```

```python
import jax
import jax.numpy as jnp
from jax import lax
from jax.experimental import pallas as pl
from jax.experimental.pallas import tpu as pltpu
from jax.sharding import Mesh, PartitionSpec as P

REP = ("x", "zl")
FSDP = ("zh", "y", "core")
REPLICAS = 12
ENTRIES = 12288 * 3072
MIB = 1024 * 1024
ANY = pl.BlockSpec(memory_space=pl.ANY)


def hbm(x):
    return pltpu.with_memory_space_constraint(x, pltpu.HBM)


def unpack_kernel(words_hbm, scales_hbm, out_hbm, order_ref, words_ref, scales_ref, out_ref, sems):
    steps, per_step, rows, _ = out_ref.shape
    span = per_step * 128
    copies_in = [pltpu.make_async_copy(scales_hbm, scales_ref, sems.at[0])]
    for i in range(steps):
        cols = pl.ds(i * span, span)
        copies_in.append(
            pltpu.make_async_copy(words_hbm.at[:, cols], words_ref.at[:, cols], sems.at[1 + i])
        )
    for copy in copies_in:
        copy.start()
    order_ref[...] = jnp.zeros(order_ref.shape, jnp.float32)
    first = lax.broadcasted_iota(jnp.int32, (rows, 128), 1) < 64
    copies_in[0].wait()
    scales = scales_ref[...].T
    copies_out = []
    for i in range(steps):
        copies_in[1 + i].wait()
        for k in range(per_step):
            c = i * per_step + k
            words = words_ref[:, c * 128 : (c + 1) * 128]
            scale = jnp.where(first, scales[:, 2 * c : 2 * c + 1], scales[:, 2 * c + 1 : 2 * c + 2])
            low = ((words & 15) - 8).astype(jnp.float32) * scale
            high = ((words >> 4) - 8).astype(jnp.float32) * scale
            out_ref[i, k, :, :128] = low.astype(jnp.bfloat16)
            out_ref[i, k, :, 128:] = high.astype(jnp.bfloat16)
        copies_out.append(pltpu.make_async_copy(out_ref.at[i], out_hbm.at[i], sems.at[1 + steps + i]))
        copies_out[-1].start()
    for copy in copies_out:
        copy.wait()


def unpack(words, scales_t):
    rows, width = words.shape
    shape = (4, REPLICAS // 4, rows, 256)
    return pl.pallas_call(
        unpack_kernel,
        in_specs=[ANY, ANY],
        out_specs=(ANY, pl.BlockSpec(memory_space=pltpu.VMEM)),
        out_shape=(
            pltpu.HBM(shape, jnp.bfloat16),
            pltpu.VMEM((8, 128), jnp.float32),
        ),
        scratch_shapes=[
            pltpu.VMEM((rows, width), jnp.int32),
            pltpu.VMEM(scales_t.shape, jnp.float32),
            pltpu.VMEM(shape, jnp.bfloat16),
            pltpu.SemaphoreType.DMA((9,)),
        ],
        compiler_params=pltpu.CompilerParams(vmem_limit_bytes=32 * MIB),
        name="unpack",
    )(hbm(words), hbm(scales_t))


def gradients_kernel(
    order_ref, gate_hbm, up_hbm, out_grad_hbm, momentum_hbm, params_hbm,
    grads_ref, total_ref, momentum_ref, params_ref,
    gate_ref, up_ref, out_grad_ref, sems,
):
    width = out_grad_ref.shape[1]
    steps = width // 512
    columns = [pl.ds(c * 512, 512) for c in range(steps)]
    first = [
        pltpu.make_async_copy(gate_hbm, gate_ref, sems.at[0]),
        pltpu.make_async_copy(up_hbm, up_ref, sems.at[1]),
    ]
    blocks = [
        pltpu.make_async_copy(out_grad_hbm.at[:, cols], out_grad_ref.at[:, cols], sems.at[2 + c])
        for c, cols in enumerate(columns)
    ]
    last = [
        pltpu.make_async_copy(momentum_hbm, momentum_ref, sems.at[2 + steps]),
        pltpu.make_async_copy(params_hbm, params_ref, sems.at[3 + steps]),
    ]
    for copy in first + blocks + last:
        copy.start()
    for copy in first:
        copy.wait()
    gate = gate_ref[...].astype(jnp.float32)
    up = up_ref[...].astype(jnp.float32)
    hidden = (gate * jax.nn.sigmoid(gate) * up).astype(jnp.bfloat16)
    tokens = gate_ref.shape[1]
    total = jnp.zeros((8, 512), jnp.float32)
    for copy, cols in zip(blocks, columns):
        copy.wait()
        part = lax.dot_general(
            hidden, out_grad_ref[:, cols], (((1,), (0,)), ((), ())), preferred_element_type=jnp.float32
        ) * (1.0 / tokens)
        grads_ref[:, cols] = part.astype(jnp.bfloat16)
        total += jnp.sum((part * part).reshape(-1, 8, 512), axis=0)
    total_ref[...] = jnp.broadcast_to(jnp.sum(total), (8, 128)) + order_ref[...]
    for copy in last:
        copy.wait()


def gradients(order, gate_t, up_t, out_grad, momentum, params):
    rows, tokens = gate_t.shape
    width = out_grad.shape[1]
    return pl.pallas_call(
        gradients_kernel,
        in_specs=[pl.BlockSpec(memory_space=pltpu.VMEM)] + [ANY] * 5,
        out_shape=(
            pltpu.VMEM((rows, width), jnp.bfloat16),
            pltpu.VMEM((8, 128), jnp.float32),
            pltpu.VMEM(momentum.shape, jnp.float32),
            pltpu.VMEM(params.shape, jnp.float32),
        ),
        scratch_shapes=[
            pltpu.VMEM((rows, tokens), jnp.bfloat16),
            pltpu.VMEM((rows, tokens), jnp.bfloat16),
            pltpu.VMEM((tokens, width), jnp.bfloat16),
            pltpu.SemaphoreType.DMA((width // 512 + 4,)),
        ],
        compiler_params=pltpu.CompilerParams(vmem_limit_bytes=32 * MIB),
        cost_estimate=pl.CostEstimate(
            flops=2 * rows * width * tokens, bytes_accessed=6_000_000, transcendentals=rows * tokens
        ),
        name="gradients",
    )(order, *map(hbm, (gate_t, up_t, out_grad, momentum, params)))


def update_kernel(parts_ref, total_ref, momentum_ref, params_ref,
                  bf_hbm, global_hbm, momentum_hbm, total_out_ref, momentum_out_ref, global_ref, bf_ref, sems):
    row = lax.broadcasted_iota(jnp.int32, (256, 256), 0)
    col = lax.broadcasted_iota(jnp.int32, (256, 256), 1)
    weave = ((row & 127) * 2 + (row >> 7) == col).astype(jnp.bfloat16)
    delta = jnp.zeros(momentum_ref.shape, jnp.float32)
    for c in range(REPLICAS):
        delta += jnp.dot(parts_ref[c], weave, preferred_element_type=jnp.float32)
    delta = delta * (1.0 / REPLICAS)
    momentum = 0.9 * momentum_ref[...] + delta
    new_global = params_ref[...] - 0.7 * (delta + 0.9 * momentum)
    bf_ref[...] = new_global.astype(jnp.bfloat16)
    copies = [pltpu.make_async_copy(bf_ref, bf_hbm.at[c], sems.at[c]) for c in range(REPLICAS)]
    for copy in copies:
        copy.start()
    momentum_out_ref[...] = momentum
    global_ref[...] = new_global
    outs = [
        pltpu.make_async_copy(momentum_out_ref, momentum_hbm, sems.at[REPLICAS]),
        pltpu.make_async_copy(global_ref, global_hbm, sems.at[REPLICAS + 1]),
    ]
    for copy in outs:
        copy.start()
    total_out_ref[...] = total_ref[...]
    for copy in copies + outs:
        copy.wait()


def update(parts, momentum, params, total):
    rows, width = momentum.shape
    vmem = pl.BlockSpec(memory_space=pltpu.VMEM)
    state = pltpu.HBM((rows, width), jnp.float32)
    return pl.pallas_call(
        update_kernel,
        out_specs=(ANY, ANY, ANY, vmem),
        out_shape=(
            pltpu.HBM((REPLICAS, rows, width), jnp.bfloat16), state, state, pltpu.VMEM((8, 128), jnp.float32)
        ),
        scratch_shapes=[
            pltpu.VMEM((rows, width), jnp.float32),
            pltpu.VMEM((rows, width), jnp.float32),
            pltpu.VMEM((rows, width), jnp.bfloat16),
            pltpu.SemaphoreType.DMA((REPLICAS + 2,)),
        ],
        compiler_params=pltpu.CompilerParams(vmem_limit_bytes=32 * MIB),
        name="update",
    )(parts, total, momentum, params)


def stage_kernel(total_ref, inner_hbm, inner_ref, total_out_ref, sem):
    copy = pltpu.make_async_copy(inner_hbm, inner_ref, sem)
    copy.start()
    total_out_ref[...] = total_ref[...]
    copy.wait()


def stage(total, inner):
    return pl.pallas_call(
        stage_kernel,
        in_specs=[pl.BlockSpec(memory_space=pltpu.VMEM), ANY],
        out_shape=(pltpu.VMEM(inner.shape, inner.dtype), pltpu.VMEM((8, 128), jnp.float32)),
        scratch_shapes=[pltpu.SemaphoreType.DMA],
        compiler_params=pltpu.CompilerParams(vmem_limit_bytes=32 * MIB),
        name="stage",
    )(total, hbm(inner))


def merge_kernel(total_ref, grads_ref, inner_ref, global_ref, out_hbm, out_ref, sems):
    root_mean = jnp.sqrt(total_ref[:1, :1] / ENTRIES + 1e-6)
    share = 0.4 * jnp.minimum(1.0, 0.02 / root_mean)
    copies = []
    for c in range(REPLICAS):
        cols = pl.ds(c * 256, 256)
        kept = 0.42 * inner_ref[:, cols].astype(jnp.float32) - share * grads_ref[:, cols].astype(jnp.float32)
        out_ref[:, cols] = (kept + 0.5 * global_ref[c].astype(jnp.float32)).astype(jnp.bfloat16)
        if c % 2 == 1:
            cols = pl.ds((c - 1) * 256, 512)
            copies.append(pltpu.make_async_copy(out_ref.at[:, cols], out_hbm.at[:, cols], sems.at[c // 2]))
            copies[-1].start()
    for copy in copies:
        copy.wait()


def merge(total, grads, inner, global_parts):
    return pl.pallas_call(
        merge_kernel,
        out_specs=ANY,
        out_shape=jax.ShapeDtypeStruct(inner.shape, jnp.bfloat16),
        scratch_shapes=[pltpu.VMEM(inner.shape, jnp.bfloat16), pltpu.SemaphoreType.DMA((6,))],
        compiler_params=pltpu.CompilerParams(vmem_limit_bytes=32 * MIB),
        name="merge",
    )(total, grads, inner, global_parts)


def per_device(gate_pre, up_pre, out_grad, inner_params, global_params, outer_momentum, pair_codes, code_scales):
    pseudo, order = unpack(pair_codes[0], code_scales[0].T)
    parts = lax.all_to_all(pseudo.reshape((REPLICAS,) + pseudo.shape[2:]), REP, 0, 0, tiled=True)
    grads, total, momentum, params = gradients(
        order, gate_pre.T, up_pre.T, out_grad, outer_momentum, global_params
    )
    total = lax.psum(lax.psum(total, "core"), "zh")
    global_bf, new_global, new_momentum, total = update(parts, momentum, params, total)
    global_parts = lax.all_to_all(global_bf, REP, 0, 0, tiled=True)
    inner, total = stage(total, inner_params[0])
    total = lax.psum(total, "y")
    merged = merge(total, grads, inner, global_parts)
    return (merged[None], new_global, new_momentum)


def solution(mesh):
    fine = Mesh(mesh.devices.reshape(4, 3, 4, 8, 2), REP + FSDP)
    in_specs = (
        P(REP, FSDP),
        P(REP, FSDP),
        P(REP, None),
        P(REP, FSDP, None),
        P(FSDP, REP),
        P(FSDP, REP),
        P(REP, FSDP, None),
        P(REP, FSDP, None),
    )
    out_specs = (P(REP, FSDP, None), P(FSDP, REP), P(FSDP, REP))
    return jax.shard_map(
        per_device, mesh=fine, in_specs=in_specs, out_specs=out_specs, check_vma=False
    )
```

```python
import functools

import jax
import jax.numpy as jnp
from jax import lax
from jax.experimental import pallas as pl
from jax.experimental.pallas import tpu as pltpu
from jax.sharding import Mesh, PartitionSpec as P

REP = ("x", "zl")
FSDP = ("zh", "y", "core")
REPLICAS = 12
ENTRIES = 12288 * 3072
MIB = 1024 * 1024
ANY = pl.BlockSpec(memory_space=pl.ANY)


def hbm(x):
    return pltpu.with_memory_space_constraint(x, pltpu.HBM)


def unpack_kernel(words_hbm, scales_hbm, after_ref, out_hbm, order_ref, words_ref, scales_ref, out_ref, sems):
    steps, per_step, rows, _ = out_ref.shape
    span = per_step * 128
    copies_in = [pltpu.make_async_copy(scales_hbm, scales_ref, sems.at[0])]
    for i in range(steps):
        cols = pl.ds(i * span, span)
        copies_in.append(
            pltpu.make_async_copy(words_hbm.at[:, cols], words_ref.at[:, cols], sems.at[1 + i])
        )
    for copy in copies_in:
        copy.start()
    order_ref[...] = jnp.zeros(order_ref.shape, jnp.float32)
    first = lax.broadcasted_iota(jnp.int32, (rows, 128), 1) < 64
    copies_in[0].wait()
    scales = scales_ref[...].T
    copies_out = []
    for i in range(steps):
        copies_in[1 + i].wait()
        for k in range(per_step):
            c = i * per_step + k
            words = words_ref[:, c * 128 : (c + 1) * 128]
            scale = jnp.where(first, scales[:, 2 * c : 2 * c + 1], scales[:, 2 * c + 1 : 2 * c + 2])
            low = ((words & 15) - 8).astype(jnp.float32) * scale
            high = ((words >> 4) - 8).astype(jnp.float32) * scale
            out_ref[i, k, :, :128] = low.astype(jnp.bfloat16)
            out_ref[i, k, :, 128:] = high.astype(jnp.bfloat16)
        copies_out.append(pltpu.make_async_copy(out_ref.at[i], out_hbm.at[i], sems.at[1 + steps + i]))
        copies_out[-1].start()
    for copy in copies_out:
        copy.wait()


def unpack(words, scales_t, after):
    rows, width = words.shape
    shape = (4, REPLICAS // 4, rows, 256)
    return pl.pallas_call(
        unpack_kernel,
        in_specs=[ANY, ANY, pl.BlockSpec(memory_space=pltpu.VMEM)],
        out_specs=(ANY, pl.BlockSpec(memory_space=pltpu.VMEM)),
        out_shape=(
            pltpu.HBM(shape, jnp.bfloat16),
            pltpu.VMEM((8, 128), jnp.float32),
        ),
        scratch_shapes=[
            pltpu.VMEM((rows, width), jnp.int32),
            pltpu.VMEM(scales_t.shape, jnp.float32),
            pltpu.VMEM(shape, jnp.bfloat16),
            pltpu.SemaphoreType.DMA((9,)),
        ],
        compiler_params=pltpu.CompilerParams(vmem_limit_bytes=32 * MIB),
        name="unpack",
    )(hbm(words), hbm(scales_t), after)


def gradients_body(
    order_ref, gate_hbm, up_hbm, out_grad_hbm, momentum_hbm, params_hbm,
    grads_ref, total_ref, momentum_ref, params_ref,
    gate_ref, up_ref, out_grad_ref, sems,
):
    width = out_grad_ref.shape[1]
    steps = width // 512
    columns = [pl.ds(c * 512, 512) for c in range(steps)]
    first = [
        pltpu.make_async_copy(gate_hbm, gate_ref, sems.at[0]),
        pltpu.make_async_copy(up_hbm, up_ref, sems.at[1]),
    ]
    blocks = [
        pltpu.make_async_copy(out_grad_hbm.at[:, cols], out_grad_ref.at[:, cols], sems.at[2 + c])
        for c, cols in enumerate(columns)
    ]
    last = [
        pltpu.make_async_copy(momentum_hbm, momentum_ref, sems.at[2 + steps]),
        pltpu.make_async_copy(params_hbm, params_ref, sems.at[3 + steps]),
    ]
    for copy in first + blocks + last:
        copy.start()
    for copy in first:
        copy.wait()
    gate = gate_ref[...].astype(jnp.float32)
    up = up_ref[...].astype(jnp.float32)
    hidden = (gate * jax.nn.sigmoid(gate) * up).astype(jnp.bfloat16)
    tokens = gate_ref.shape[1]
    total = jnp.zeros((8, 512), jnp.float32)
    for copy, cols in zip(blocks, columns):
        copy.wait()
        part = lax.dot_general(
            hidden, out_grad_ref[:, cols], (((1,), (0,)), ((), ())), preferred_element_type=jnp.float32
        ) * (1.0 / tokens)
        grads_ref[:, cols] = part.astype(jnp.bfloat16)
        total += jnp.sum((part * part).reshape(-1, 8, 512), axis=0)
    total_ref[...] = jnp.broadcast_to(jnp.sum(total), (8, 128)) + order_ref[...]
    for copy in last:
        copy.wait()


def gradients_kernel(core, order_ref, *refs):
    if core == 1:
        refs = refs[4:]

    @pl.when(lax.axis_index("core") == core)
    def _():
        gradients_body(order_ref, *refs)


def gradients(core, order, earlier, gate_t, up_t, out_grad, momentum, params):
    rows, tokens = gate_t.shape
    width = out_grad.shape[1]
    return pl.pallas_call(
        functools.partial(gradients_kernel, core),
        in_specs=[pl.BlockSpec(memory_space=pltpu.VMEM)] * (1 + len(earlier)) + [ANY] * 5,
        input_output_aliases={1 + i: i for i in range(len(earlier))},
        out_shape=(
            pltpu.VMEM((rows, width), jnp.bfloat16),
            pltpu.VMEM((8, 128), jnp.float32),
            pltpu.VMEM(momentum.shape, jnp.float32),
            pltpu.VMEM(params.shape, jnp.float32),
        ),
        scratch_shapes=[
            pltpu.VMEM((rows, tokens), jnp.bfloat16),
            pltpu.VMEM((rows, tokens), jnp.bfloat16),
            pltpu.VMEM((tokens, width), jnp.bfloat16),
            pltpu.SemaphoreType.DMA((width // 512 + 4,)),
        ],
        compiler_params=pltpu.CompilerParams(vmem_limit_bytes=32 * MIB),
        cost_estimate=pl.CostEstimate(
            flops=2 * rows * width * tokens, bytes_accessed=6_000_000, transcendentals=rows * tokens
        ),
        name="gradients",
    )(order, *earlier, *map(hbm, (gate_t, up_t, out_grad, momentum, params)))


def update_kernel(parts_ref, total_ref, momentum_ref, params_ref,
                  bf_hbm, global_hbm, momentum_hbm, total_out_ref, momentum_out_ref, global_ref, bf_ref, sems):
    row = lax.broadcasted_iota(jnp.int32, (256, 256), 0)
    col = lax.broadcasted_iota(jnp.int32, (256, 256), 1)
    weave = ((row & 127) * 2 + (row >> 7) == col).astype(jnp.bfloat16)
    delta = jnp.zeros(momentum_ref.shape, jnp.float32)
    for c in range(REPLICAS):
        delta += jnp.dot(parts_ref[c], weave, preferred_element_type=jnp.float32)
    delta = delta * (1.0 / REPLICAS)
    momentum = 0.9 * momentum_ref[...] + delta
    new_global = params_ref[...] - 0.7 * (delta + 0.9 * momentum)
    bf_ref[...] = new_global.astype(jnp.bfloat16)
    copies = [pltpu.make_async_copy(bf_ref, bf_hbm.at[c], sems.at[c]) for c in range(REPLICAS)]
    for copy in copies:
        copy.start()
    momentum_out_ref[...] = momentum
    global_ref[...] = new_global
    outs = [
        pltpu.make_async_copy(momentum_out_ref, momentum_hbm, sems.at[REPLICAS]),
        pltpu.make_async_copy(global_ref, global_hbm, sems.at[REPLICAS + 1]),
    ]
    for copy in outs:
        copy.start()
    total_out_ref[...] = total_ref[...]
    for copy in copies + outs:
        copy.wait()


def update(parts, momentum, params, total):
    rows, width = momentum.shape
    vmem = pl.BlockSpec(memory_space=pltpu.VMEM)
    state = pltpu.HBM((rows, width), jnp.float32)
    return pl.pallas_call(
        update_kernel,
        out_specs=(ANY, ANY, ANY, vmem),
        out_shape=(
            pltpu.HBM((REPLICAS, rows, width), jnp.bfloat16), state, state, pltpu.VMEM((8, 128), jnp.float32)
        ),
        scratch_shapes=[
            pltpu.VMEM((rows, width), jnp.float32),
            pltpu.VMEM((rows, width), jnp.float32),
            pltpu.VMEM((rows, width), jnp.bfloat16),
            pltpu.SemaphoreType.DMA((REPLICAS + 2,)),
        ],
        compiler_params=pltpu.CompilerParams(vmem_limit_bytes=32 * MIB),
        name="update",
    )(parts, total, momentum, params)


def stage_kernel(total_ref, inner_hbm, inner_ref, total_out_ref, sem):
    copy = pltpu.make_async_copy(inner_hbm, inner_ref, sem)
    copy.start()
    total_out_ref[...] = total_ref[...]
    copy.wait()


def stage(total, inner):
    return pl.pallas_call(
        stage_kernel,
        in_specs=[pl.BlockSpec(memory_space=pltpu.VMEM), ANY],
        out_shape=(pltpu.VMEM(inner.shape, inner.dtype), pltpu.VMEM((8, 128), jnp.float32)),
        scratch_shapes=[pltpu.SemaphoreType.DMA],
        compiler_params=pltpu.CompilerParams(vmem_limit_bytes=32 * MIB),
        name="stage",
    )(total, hbm(inner))


def merge_kernel(total_ref, grads_ref, inner_ref, global_ref, out_hbm, out_ref, sems):
    root_mean = jnp.sqrt(total_ref[:1, :1] / ENTRIES + 1e-6)
    share = 0.4 * jnp.minimum(1.0, 0.02 / root_mean)
    copies = []
    for c in range(REPLICAS):
        cols = pl.ds(c * 256, 256)
        kept = 0.42 * inner_ref[:, cols].astype(jnp.float32) - share * grads_ref[:, cols].astype(jnp.float32)
        out_ref[:, cols] = (kept + 0.5 * global_ref[c].astype(jnp.float32)).astype(jnp.bfloat16)
        if c % 2 == 1:
            cols = pl.ds((c - 1) * 256, 512)
            copies.append(pltpu.make_async_copy(out_ref.at[:, cols], out_hbm.at[:, cols], sems.at[c // 2]))
            copies[-1].start()
    for copy in copies:
        copy.wait()


def merge(total, grads, inner, global_parts):
    return pl.pallas_call(
        merge_kernel,
        out_specs=ANY,
        out_shape=jax.ShapeDtypeStruct(inner.shape, jnp.bfloat16),
        scratch_shapes=[pltpu.VMEM(inner.shape, jnp.bfloat16), pltpu.SemaphoreType.DMA((6,))],
        compiler_params=pltpu.CompilerParams(vmem_limit_bytes=32 * MIB),
        name="merge",
    )(total, grads, inner, global_parts)


def run_sum(total):
    zh, y = lax.axis_size("zh"), lax.axis_size("y")
    groups = [[2 * (i * y + j) + 1 for i in range(zh)] for j in range(y)]
    groups += [[2 * (i * y + j + k) for k in range(zh)] for i in range(zh) for j in range(0, y, zh)]
    total = lax.psum(total, FSDP, axis_index_groups=groups)
    return jnp.where(lax.axis_index("core") == 1, total, 0.0)


def crossed_sum(total, axis):
    n = lax.axis_size(axis)
    groups = [[2 * i + (i + p) % 2 for i in range(n)] for p in range(2)]
    return lax.psum(total, (axis, "core"), axis_index_groups=groups)


def per_device(gate_pre, up_pre, out_grad, inner_params, global_params, outer_momentum, pair_codes, code_scales):
    operands = (gate_pre.T, up_pre.T, out_grad, outer_momentum, global_params)
    early = gradients(0, jnp.zeros((8, 128), jnp.float32), (), *operands)
    pseudo, order = unpack(pair_codes[0], code_scales[0].T, early[1])
    parts = lax.all_to_all(pseudo.reshape((REPLICAS,) + pseudo.shape[2:]), REP, 0, 0, tiled=True)
    grads, total, momentum, params = gradients(1, order, early, *operands)
    total = run_sum(lax.psum(total, "core"))
    global_bf, new_global, new_momentum, total = update(parts, momentum, params, total)
    global_parts = lax.all_to_all(global_bf, REP, 0, 0, tiled=True)
    inner, total = stage(total, inner_params[0])
    total = crossed_sum(lax.psum(total, "core"), "y")
    merged = merge(total, grads, inner, global_parts)
    return (merged[None], new_global, new_momentum)


def solution(mesh):
    fine = Mesh(mesh.devices.reshape(4, 3, 4, 8, 2), REP + FSDP)
    in_specs = (
        P(REP, FSDP),
        P(REP, FSDP),
        P(REP, None),
        P(REP, FSDP, None),
        P(FSDP, REP),
        P(FSDP, REP),
        P(REP, FSDP, None),
        P(REP, FSDP, None),
    )
    out_specs = (P(REP, FSDP, None), P(FSDP, REP), P(FSDP, REP))
    return jax.shard_map(
        per_device, mesh=fine, in_specs=in_specs, out_specs=out_specs, check_vma=False
    )
```

```python
import functools

import jax
import jax.numpy as jnp
from jax import lax
from jax.experimental import pallas as pl
from jax.experimental.pallas import tpu as pltpu
from jax.sharding import Mesh, PartitionSpec as P

REP = ("x", "zl")
FSDP = ("zh", "y", "core")
REPLICAS = 12
ENTRIES = 12288 * 3072
MIB = 1024 * 1024
ANY = pl.BlockSpec(memory_space=pl.ANY)


def hbm(x):
    return pltpu.with_memory_space_constraint(x, pltpu.HBM)


def unpack_kernel(words_hbm, scales_hbm, after_ref, out_hbm, order_ref, words_ref, scales_ref, out_ref, sems):
    steps, per_step, rows, _ = out_ref.shape
    span = per_step * 128
    copies_in = [pltpu.make_async_copy(scales_hbm, scales_ref, sems.at[0])]
    for i in range(steps):
        cols = pl.ds(i * span, span)
        copies_in.append(
            pltpu.make_async_copy(words_hbm.at[:, cols], words_ref.at[:, cols], sems.at[1 + i])
        )
    for copy in copies_in:
        copy.start()
    order_ref[...] = jnp.zeros(order_ref.shape, jnp.float32)
    first = lax.broadcasted_iota(jnp.int32, (rows, 128), 1) < 64
    copies_in[0].wait()
    scales = scales_ref[...].T
    copies_out = []
    for i in range(steps):
        copies_in[1 + i].wait()
        for k in range(per_step):
            c = i * per_step + k
            words = words_ref[:, c * 128 : (c + 1) * 128]
            scale = jnp.where(first, scales[:, 2 * c : 2 * c + 1], scales[:, 2 * c + 1 : 2 * c + 2])
            low = ((words & 15) - 8).astype(jnp.float32) * scale
            high = ((words >> 4) - 8).astype(jnp.float32) * scale
            out_ref[i, k, :, :128] = low.astype(jnp.bfloat16)
            out_ref[i, k, :, 128:] = high.astype(jnp.bfloat16)
        copies_out.append(pltpu.make_async_copy(out_ref.at[i], out_hbm.at[i], sems.at[1 + steps + i]))
        copies_out[-1].start()
    for copy in copies_out:
        copy.wait()


def unpack(words, scales_t, after):
    rows, width = words.shape
    shape = (4, REPLICAS // 4, rows, 256)
    return pl.pallas_call(
        unpack_kernel,
        in_specs=[ANY, ANY, pl.BlockSpec(memory_space=pltpu.VMEM)],
        out_specs=(ANY, pl.BlockSpec(memory_space=pltpu.VMEM)),
        out_shape=(
            pltpu.HBM(shape, jnp.bfloat16),
            pltpu.VMEM((8, 128), jnp.float32),
        ),
        scratch_shapes=[
            pltpu.VMEM((rows, width), jnp.int32),
            pltpu.VMEM(scales_t.shape, jnp.float32),
            pltpu.VMEM(shape, jnp.bfloat16),
            pltpu.SemaphoreType.DMA((9,)),
        ],
        compiler_params=pltpu.CompilerParams(vmem_limit_bytes=32 * MIB),
        name="unpack",
    )(hbm(words), hbm(scales_t), after)


def gradients_body(
    order_ref, gate_hbm, up_hbm, out_grad_hbm, momentum_hbm, params_hbm,
    grads_ref, total_ref, momentum_ref, params_ref,
    gate_ref, up_ref, out_grad_ref, sems,
):
    width = out_grad_ref.shape[1]
    steps = width // 512
    columns = [pl.ds(c * 512, 512) for c in range(steps)]
    first = [
        pltpu.make_async_copy(gate_hbm, gate_ref, sems.at[0]),
        pltpu.make_async_copy(up_hbm, up_ref, sems.at[1]),
    ]
    blocks = [
        pltpu.make_async_copy(out_grad_hbm.at[:, cols], out_grad_ref.at[:, cols], sems.at[2 + c])
        for c, cols in enumerate(columns)
    ]
    last = [
        pltpu.make_async_copy(momentum_hbm, momentum_ref, sems.at[2 + steps]),
        pltpu.make_async_copy(params_hbm, params_ref, sems.at[3 + steps]),
    ]
    for copy in first + blocks + last:
        copy.start()
    for copy in first:
        copy.wait()
    gate = gate_ref[...].astype(jnp.float32)
    up = up_ref[...].astype(jnp.float32)
    hidden = (gate * jax.nn.sigmoid(gate) * up).astype(jnp.bfloat16)
    tokens = gate_ref.shape[1]
    total = jnp.zeros((8, 512), jnp.float32)
    for copy, cols in zip(blocks, columns):
        copy.wait()
        part = lax.dot_general(
            hidden, out_grad_ref[:, cols], (((1,), (0,)), ((), ())), preferred_element_type=jnp.float32
        ) * (1.0 / tokens)
        grads_ref[:, cols] = part.astype(jnp.bfloat16)
        total += jnp.sum((part * part).reshape(-1, 8, 512), axis=0)
    total_ref[...] = jnp.broadcast_to(jnp.sum(total), (8, 128)) + order_ref[...]
    for copy in last:
        copy.wait()


def gradients_kernel(core, order_ref, *refs):
    if core == 1:
        refs = refs[4:]

    @pl.when(lax.axis_index("core") == core)
    def _():
        gradients_body(order_ref, *refs)


def gradients(core, order, earlier, gate_t, up_t, out_grad, momentum, params):
    rows, tokens = gate_t.shape
    width = out_grad.shape[1]
    return pl.pallas_call(
        functools.partial(gradients_kernel, core),
        in_specs=[pl.BlockSpec(memory_space=pltpu.VMEM)] * (1 + len(earlier)) + [ANY] * 5,
        input_output_aliases={1 + i: i for i in range(len(earlier))},
        out_shape=(
            pltpu.VMEM((rows, width), jnp.bfloat16),
            pltpu.VMEM((8, 128), jnp.float32),
            pltpu.VMEM(momentum.shape, jnp.float32),
            pltpu.VMEM(params.shape, jnp.float32),
        ),
        scratch_shapes=[
            pltpu.VMEM((rows, tokens), jnp.bfloat16),
            pltpu.VMEM((rows, tokens), jnp.bfloat16),
            pltpu.VMEM((tokens, width), jnp.bfloat16),
            pltpu.SemaphoreType.DMA((width // 512 + 4,)),
        ],
        compiler_params=pltpu.CompilerParams(vmem_limit_bytes=32 * MIB),
        cost_estimate=pl.CostEstimate(
            flops=2 * rows * width * tokens, bytes_accessed=6_000_000, transcendentals=rows * tokens
        ),
        name="gradients",
    )(order, *earlier, *map(hbm, (gate_t, up_t, out_grad, momentum, params)))


def update_kernel(parts_ref, total_ref, momentum_ref, params_ref,
                  bf_hbm, global_hbm, momentum_hbm, total_out_ref, momentum_out_ref, global_ref, bf_ref, sems):
    row = lax.broadcasted_iota(jnp.int32, (256, 256), 0)
    col = lax.broadcasted_iota(jnp.int32, (256, 256), 1)
    weave = ((row & 127) * 2 + (row >> 7) == col).astype(jnp.bfloat16)
    delta = jnp.zeros(momentum_ref.shape, jnp.float32)
    for c in range(REPLICAS):
        delta += jnp.dot(parts_ref[c], weave, preferred_element_type=jnp.float32)
    delta = delta * (1.0 / REPLICAS)
    momentum = 0.9 * momentum_ref[...] + delta
    new_global = params_ref[...] - 0.7 * (delta + 0.9 * momentum)
    bf_ref[...] = new_global.astype(jnp.bfloat16)
    copies = [pltpu.make_async_copy(bf_ref, bf_hbm.at[c], sems.at[c]) for c in range(REPLICAS)]
    for copy in copies:
        copy.start()
    momentum_out_ref[...] = momentum
    global_ref[...] = new_global
    outs = [
        pltpu.make_async_copy(momentum_out_ref, momentum_hbm, sems.at[REPLICAS]),
        pltpu.make_async_copy(global_ref, global_hbm, sems.at[REPLICAS + 1]),
    ]
    for copy in outs:
        copy.start()
    total_out_ref[...] = total_ref[...]
    for copy in copies + outs:
        copy.wait()


def update(parts, momentum, params, total):
    rows, width = momentum.shape
    vmem = pl.BlockSpec(memory_space=pltpu.VMEM)
    state = pltpu.HBM((rows, width), jnp.float32)
    return pl.pallas_call(
        update_kernel,
        out_specs=(ANY, ANY, ANY, vmem),
        out_shape=(
            pltpu.HBM((REPLICAS, rows, width), jnp.bfloat16), state, state, pltpu.VMEM((8, 128), jnp.float32)
        ),
        scratch_shapes=[
            pltpu.VMEM((rows, width), jnp.float32),
            pltpu.VMEM((rows, width), jnp.float32),
            pltpu.VMEM((rows, width), jnp.bfloat16),
            pltpu.SemaphoreType.DMA((REPLICAS + 2,)),
        ],
        compiler_params=pltpu.CompilerParams(vmem_limit_bytes=32 * MIB),
        name="update",
    )(parts, total, momentum, params)


def stage_kernel(total_ref, inner_hbm, inner_ref, total_out_ref, sem):
    copy = pltpu.make_async_copy(inner_hbm, inner_ref, sem)
    copy.start()
    total_out_ref[...] = total_ref[...]
    copy.wait()


def stage(total, inner):
    return pl.pallas_call(
        stage_kernel,
        in_specs=[pl.BlockSpec(memory_space=pltpu.VMEM), ANY],
        out_shape=(pltpu.VMEM(inner.shape, inner.dtype), pltpu.VMEM((8, 128), jnp.float32)),
        scratch_shapes=[pltpu.SemaphoreType.DMA],
        compiler_params=pltpu.CompilerParams(vmem_limit_bytes=32 * MIB),
        name="stage",
    )(total, hbm(inner))


def merge_kernel(total_ref, grads_ref, inner_ref, global_ref, out_hbm, out_ref, sems):
    root_mean = jnp.sqrt(total_ref[:1, :1] / ENTRIES + 1e-6)
    share = 0.4 * jnp.minimum(1.0, 0.02 / root_mean)
    copies = []
    for c in range(REPLICAS):
        cols = pl.ds(c * 256, 256)
        kept = 0.42 * inner_ref[:, cols].astype(jnp.float32) - share * grads_ref[:, cols].astype(jnp.float32)
        out_ref[:, cols] = (kept + 0.5 * global_ref[c].astype(jnp.float32)).astype(jnp.bfloat16)
        if c % 2 == 1:
            cols = pl.ds((c - 1) * 256, 512)
            copies.append(pltpu.make_async_copy(out_ref.at[:, cols], out_hbm.at[:, cols], sems.at[c // 2]))
            copies[-1].start()
    for copy in copies:
        copy.wait()


def merge(total, grads, inner, global_parts):
    return pl.pallas_call(
        merge_kernel,
        out_specs=ANY,
        out_shape=jax.ShapeDtypeStruct(inner.shape, jnp.bfloat16),
        scratch_shapes=[pltpu.VMEM(inner.shape, jnp.bfloat16), pltpu.SemaphoreType.DMA((6,))],
        compiler_params=pltpu.CompilerParams(vmem_limit_bytes=32 * MIB),
        name="merge",
    )(total, grads, inner, global_parts)


def run_sum(total):
    zh, y = lax.axis_size("zh"), lax.axis_size("y")
    groups = [[2 * (i * y + j) + 1 for i in range(zh)] for j in range(y)]
    groups += [[2 * (i * y + j + k) for k in range(zh)] for i in range(zh) for j in range(0, y, zh)]
    return lax.psum(total, FSDP, axis_index_groups=groups)


def per_device(gate_pre, up_pre, out_grad, inner_params, global_params, outer_momentum, pair_codes, code_scales):
    operands = (gate_pre.T, up_pre.T, out_grad, outer_momentum, global_params)
    early = gradients(0, jnp.zeros((8, 128), jnp.float32), (), *operands)
    pseudo, order = unpack(pair_codes[0], code_scales[0].T, early[1])
    parts = lax.all_to_all(pseudo.reshape((REPLICAS,) + pseudo.shape[2:]), REP, 0, 0, tiled=True)
    grads, total, momentum, params = gradients(1, order, early, *operands)
    total = run_sum(lax.psum(total, "core"))
    global_bf, new_global, new_momentum, total = update(parts, momentum, params, total)
    global_parts = lax.all_to_all(global_bf, REP, 0, 0, tiled=True)
    inner, total = stage(total, inner_params[0])
    total = jnp.where(lax.axis_index("core") == 1, lax.psum(total, "y"), 0.0)
    total = lax.psum(total, "core")
    merged = merge(total, grads, inner, global_parts)
    return (merged[None], new_global, new_momentum)


def solution(mesh):
    fine = Mesh(mesh.devices.reshape(4, 3, 4, 8, 2), REP + FSDP)
    in_specs = (
        P(REP, FSDP),
        P(REP, FSDP),
        P(REP, None),
        P(REP, FSDP, None),
        P(FSDP, REP),
        P(FSDP, REP),
        P(REP, FSDP, None),
        P(REP, FSDP, None),
    )
    out_specs = (P(REP, FSDP, None), P(FSDP, REP), P(FSDP, REP))
    return jax.shard_map(
        per_device, mesh=fine, in_specs=in_specs, out_specs=out_specs, check_vma=False
    )
```

```python
import functools

import jax
import jax.numpy as jnp
from jax import lax
from jax.experimental import pallas as pl
from jax.experimental.pallas import tpu as pltpu
from jax.sharding import Mesh, PartitionSpec as P

REP = ("x", "zl")
FSDP = ("zh", "y", "core")
REPLICAS = 12
ENTRIES = 12288 * 3072
MIB = 1024 * 1024
ANY = pl.BlockSpec(memory_space=pl.ANY)


def hbm(x):
    return pltpu.with_memory_space_constraint(x, pltpu.HBM)


def unpack_kernel(words_hbm, scales_hbm, after_ref, out_hbm, order_ref, words_ref, scales_ref, out_ref, sems):
    steps, per_step, rows, _ = out_ref.shape
    span = per_step * 128
    copies_in = [pltpu.make_async_copy(scales_hbm, scales_ref, sems.at[0])]
    for i in range(steps):
        cols = pl.ds(i * span, span)
        copies_in.append(
            pltpu.make_async_copy(words_hbm.at[:, cols], words_ref.at[:, cols], sems.at[1 + i])
        )
    for copy in copies_in:
        copy.start()
    order_ref[...] = jnp.zeros(order_ref.shape, jnp.float32)
    first = lax.broadcasted_iota(jnp.int32, (rows, 128), 1) < 64
    copies_in[0].wait()
    scales = scales_ref[...].T
    copies_out = []
    for i in range(steps):
        copies_in[1 + i].wait()
        for k in range(per_step):
            c = i * per_step + k
            words = words_ref[:, c * 128 : (c + 1) * 128]
            scale = jnp.where(first, scales[:, 2 * c : 2 * c + 1], scales[:, 2 * c + 1 : 2 * c + 2])
            low = ((words & 15) - 8).astype(jnp.float32) * scale
            high = ((words >> 4) - 8).astype(jnp.float32) * scale
            out_ref[i, k, :, :128] = low.astype(jnp.bfloat16)
            out_ref[i, k, :, 128:] = high.astype(jnp.bfloat16)
        copies_out.append(pltpu.make_async_copy(out_ref.at[i], out_hbm.at[i], sems.at[1 + steps + i]))
        copies_out[-1].start()
    for copy in copies_out:
        copy.wait()


def unpack(words, scales_t, after):
    rows, width = words.shape
    shape = (4, REPLICAS // 4, rows, 256)
    return pl.pallas_call(
        unpack_kernel,
        in_specs=[ANY, ANY, pl.BlockSpec(memory_space=pltpu.VMEM)],
        out_specs=(ANY, pl.BlockSpec(memory_space=pltpu.VMEM)),
        out_shape=(
            pltpu.HBM(shape, jnp.bfloat16),
            pltpu.VMEM((8, 128), jnp.float32),
        ),
        scratch_shapes=[
            pltpu.VMEM((rows, width), jnp.int32),
            pltpu.VMEM(scales_t.shape, jnp.float32),
            pltpu.VMEM(shape, jnp.bfloat16),
            pltpu.SemaphoreType.DMA((9,)),
        ],
        compiler_params=pltpu.CompilerParams(vmem_limit_bytes=32 * MIB),
        name="unpack",
    )(hbm(words), hbm(scales_t), after)


def gradients_body(
    order_ref, gate_hbm, up_hbm, out_grad_hbm, momentum_hbm, params_hbm,
    grads_ref, total_ref, momentum_ref, params_ref,
    gate_ref, up_ref, out_grad_ref, sems,
):
    width = out_grad_ref.shape[1]
    steps = width // 512
    columns = [pl.ds(c * 512, 512) for c in range(steps)]
    first = [
        pltpu.make_async_copy(gate_hbm, gate_ref, sems.at[0]),
        pltpu.make_async_copy(up_hbm, up_ref, sems.at[1]),
    ]
    blocks = [
        pltpu.make_async_copy(out_grad_hbm.at[:, cols], out_grad_ref.at[:, cols], sems.at[2 + c])
        for c, cols in enumerate(columns)
    ]
    last = [
        pltpu.make_async_copy(momentum_hbm, momentum_ref, sems.at[2 + steps]),
        pltpu.make_async_copy(params_hbm, params_ref, sems.at[3 + steps]),
    ]
    for copy in first + blocks + last:
        copy.start()
    for copy in first:
        copy.wait()
    gate = gate_ref[...].astype(jnp.float32)
    up = up_ref[...].astype(jnp.float32)
    hidden = (gate * jax.nn.sigmoid(gate) * up).astype(jnp.bfloat16)
    tokens = gate_ref.shape[1]
    total = jnp.zeros((8, 512), jnp.float32)
    for copy, cols in zip(blocks, columns):
        copy.wait()
        part = lax.dot_general(
            hidden, out_grad_ref[:, cols], (((1,), (0,)), ((), ())), preferred_element_type=jnp.float32
        ) * (1.0 / tokens)
        grads_ref[:, cols] = part.astype(jnp.bfloat16)
        total += jnp.sum((part * part).reshape(-1, 8, 512), axis=0)
    total_ref[...] = jnp.broadcast_to(jnp.sum(total), (8, 128)) + order_ref[...]
    for copy in last:
        copy.wait()


def gradients_kernel(core, order_ref, *refs):
    if core == 1:
        refs = refs[4:]

    @pl.when(lax.axis_index("core") == core)
    def _():
        gradients_body(order_ref, *refs)


def gradients(core, order, earlier, gate_t, up_t, out_grad, momentum, params):
    rows, tokens = gate_t.shape
    width = out_grad.shape[1]
    return pl.pallas_call(
        functools.partial(gradients_kernel, core),
        in_specs=[pl.BlockSpec(memory_space=pltpu.VMEM)] * (1 + len(earlier)) + [ANY] * 5,
        input_output_aliases={1 + i: i for i in range(len(earlier))},
        out_shape=(
            pltpu.VMEM((rows, width), jnp.bfloat16),
            pltpu.VMEM((8, 128), jnp.float32),
            pltpu.VMEM(momentum.shape, jnp.float32),
            pltpu.VMEM(params.shape, jnp.float32),
        ),
        scratch_shapes=[
            pltpu.VMEM((rows, tokens), jnp.bfloat16),
            pltpu.VMEM((rows, tokens), jnp.bfloat16),
            pltpu.VMEM((tokens, width), jnp.bfloat16),
            pltpu.SemaphoreType.DMA((width // 512 + 4,)),
        ],
        compiler_params=pltpu.CompilerParams(vmem_limit_bytes=32 * MIB),
        cost_estimate=pl.CostEstimate(
            flops=2 * rows * width * tokens, bytes_accessed=6_000_000, transcendentals=rows * tokens
        ),
        name="gradients",
    )(order, *earlier, *map(hbm, (gate_t, up_t, out_grad, momentum, params)))


def update_kernel(parts_ref, total_ref, momentum_ref, params_ref,
                  bf_hbm, global_hbm, momentum_hbm, total_out_ref, momentum_out_ref, global_ref, bf_ref, sems):
    row = lax.broadcasted_iota(jnp.int32, (256, 256), 0)
    col = lax.broadcasted_iota(jnp.int32, (256, 256), 1)
    weave = ((row & 127) * 2 + (row >> 7) == col).astype(jnp.bfloat16)
    half = bf_ref.shape[0] // 2
    copies = []
    for h in range(2):
        rows = pl.ds(h * half, half)
        delta = jnp.zeros((half, momentum_ref.shape[1]), jnp.float32)
        for c in range(REPLICAS):
            delta += jnp.dot(parts_ref[c, rows, :], weave, preferred_element_type=jnp.float32)
        delta = delta * (1.0 / REPLICAS)
        momentum = 0.9 * momentum_ref[rows, :] + delta
        new_global = params_ref[rows, :] - 0.7 * (delta + 0.9 * momentum)
        bf_ref[rows, :] = new_global.astype(jnp.bfloat16)
        sent = [
            pltpu.make_async_copy(bf_ref.at[rows, :], bf_hbm.at[c, rows, :], sems.at[h * REPLICAS + c])
            for c in range(REPLICAS)
        ]
        for copy in sent:
            copy.start()
        copies += sent
        momentum_out_ref[rows, :] = momentum
        global_ref[rows, :] = new_global
    outs = [
        pltpu.make_async_copy(momentum_out_ref, momentum_hbm, sems.at[2 * REPLICAS]),
        pltpu.make_async_copy(global_ref, global_hbm, sems.at[2 * REPLICAS + 1]),
    ]
    for copy in outs:
        copy.start()
    total_out_ref[...] = total_ref[...]
    for copy in copies + outs:
        copy.wait()


def update(parts, momentum, params, total):
    rows, width = momentum.shape
    vmem = pl.BlockSpec(memory_space=pltpu.VMEM)
    state = pltpu.HBM((rows, width), jnp.float32)
    return pl.pallas_call(
        update_kernel,
        out_specs=(ANY, ANY, ANY, vmem),
        out_shape=(
            pltpu.HBM((REPLICAS, rows, width), jnp.bfloat16), state, state, pltpu.VMEM((8, 128), jnp.float32)
        ),
        scratch_shapes=[
            pltpu.VMEM((rows, width), jnp.float32),
            pltpu.VMEM((rows, width), jnp.float32),
            pltpu.VMEM((rows, width), jnp.bfloat16),
            pltpu.SemaphoreType.DMA((2 * REPLICAS + 2,)),
        ],
        compiler_params=pltpu.CompilerParams(vmem_limit_bytes=32 * MIB),
        name="update",
    )(parts, total, momentum, params)


def stage_kernel(total_ref, inner_hbm, inner_ref, total_out_ref, sem):
    copy = pltpu.make_async_copy(inner_hbm, inner_ref, sem)
    copy.start()
    total_out_ref[...] = total_ref[...]
    copy.wait()


def stage(total, inner):
    return pl.pallas_call(
        stage_kernel,
        in_specs=[pl.BlockSpec(memory_space=pltpu.VMEM), ANY],
        out_shape=(pltpu.VMEM(inner.shape, inner.dtype), pltpu.VMEM((8, 128), jnp.float32)),
        scratch_shapes=[pltpu.SemaphoreType.DMA],
        compiler_params=pltpu.CompilerParams(vmem_limit_bytes=32 * MIB),
        name="stage",
    )(total, hbm(inner))


def merge_kernel(total_ref, grads_ref, inner_ref, global_ref, out_hbm, out_ref, sems):
    root_mean = jnp.sqrt(total_ref[:1, :1] / ENTRIES + 1e-6)
    share = 0.4 * jnp.minimum(1.0, 0.02 / root_mean)
    copies = []
    for c in range(REPLICAS):
        cols = pl.ds(c * 256, 256)
        kept = 0.42 * inner_ref[:, cols].astype(jnp.float32) - share * grads_ref[:, cols].astype(jnp.float32)
        out_ref[:, cols] = (kept + 0.5 * global_ref[c].astype(jnp.float32)).astype(jnp.bfloat16)
        if c % 2 == 1:
            cols = pl.ds((c - 1) * 256, 512)
            copies.append(pltpu.make_async_copy(out_ref.at[:, cols], out_hbm.at[:, cols], sems.at[c // 2]))
            copies[-1].start()
    for copy in copies:
        copy.wait()


def merge(total, grads, inner, global_parts):
    return pl.pallas_call(
        merge_kernel,
        out_specs=ANY,
        out_shape=jax.ShapeDtypeStruct(inner.shape, jnp.bfloat16),
        scratch_shapes=[pltpu.VMEM(inner.shape, jnp.bfloat16), pltpu.SemaphoreType.DMA((6,))],
        compiler_params=pltpu.CompilerParams(vmem_limit_bytes=32 * MIB),
        name="merge",
    )(total, grads, inner, global_parts)


def run_sum(total):
    zh, y = lax.axis_size("zh"), lax.axis_size("y")
    groups = [[2 * (i * y + j) + 1 for i in range(zh)] for j in range(y)]
    groups += [[2 * (i * y + j + k) for k in range(zh)] for i in range(zh) for j in range(0, y, zh)]
    return lax.psum(total, FSDP, axis_index_groups=groups)


def per_device(gate_pre, up_pre, out_grad, inner_params, global_params, outer_momentum, pair_codes, code_scales):
    operands = (gate_pre.T, up_pre.T, out_grad, outer_momentum, global_params)
    early = gradients(0, jnp.zeros((8, 128), jnp.float32), (), *operands)
    pseudo, order = unpack(pair_codes[0], code_scales[0].T, early[1])
    parts = lax.all_to_all(pseudo.reshape((REPLICAS,) + pseudo.shape[2:]), REP, 0, 0, tiled=True)
    grads, total, momentum, params = gradients(1, order, early, *operands)
    total = run_sum(lax.psum(total, "core"))
    global_bf, new_global, new_momentum, total = update(parts, momentum, params, total)
    global_parts = lax.all_to_all(global_bf, REP, 0, 0, tiled=True)
    inner, total = stage(total, inner_params[0])
    total = jnp.where(lax.axis_index("core") == 1, lax.psum(total, "y"), 0.0)
    total = lax.psum(total, "core")
    merged = merge(total, grads, inner, global_parts)
    return (merged[None], new_global, new_momentum)


def solution(mesh):
    fine = Mesh(mesh.devices.reshape(4, 3, 4, 8, 2), REP + FSDP)
    in_specs = (
        P(REP, FSDP),
        P(REP, FSDP),
        P(REP, None),
        P(REP, FSDP, None),
        P(FSDP, REP),
        P(FSDP, REP),
        P(REP, FSDP, None),
        P(REP, FSDP, None),
    )
    out_specs = (P(REP, FSDP, None), P(FSDP, REP), P(FSDP, REP))
    return jax.shard_map(
        per_device, mesh=fine, in_specs=in_specs, out_specs=out_specs, check_vma=False
    )
```
